32 devices in a mesh: groups: 2 (over y), ctx: 4 (over z), head: 2 (over x), sub: 2 (over core).
Axes of the slice: x: 2, y: 2, z: 4, core: 2. Of those that a mesh axis runs over, the one named last changes fastest.
Arguments:
- queries: bfloat16 [16384, 4096], P(('groups', 'ctx', 'sub'), 'head'), parts along dimension 0, may hold values from -6 to 6
- keys: bfloat16 [16384, 4096], P(('groups', 'ctx', 'sub'), 'head'), parts along dimension 0, may hold values from -6 to 6
- values: bfloat16 [16384, 4096], P(('groups', 'ctx', 'sub'), 'head'), parts along dimension 0, may hold values from -6 to 6
- out_weight: bfloat16 [4096, 4096], P('head', ('ctx', 'sub')), may hold values from -0.09375 to 0.09375
- norm_gain: float32 [4096], P('head'), may hold values from 0.1 to 1.9
Outputs:
- layer_out: bfloat16 [16384, 4096], P(('groups', 'ctx', 'sub'), 'head'), parts along dimension 0
The draws below stay inside these ranges and needn't reach their ends.
There are 2 independent parts, one for each index of `groups`. The reference program is written for one: setup_inputs(seed, part) draws one part's arguments, and reference() takes and returns one part's arrays. A program takes and returns all parts, laid end to end along the dimension named above; an argument that names none is the same for every part. Nothing has to cross between parts.
All inputs are finite; a program needn't handle non-finite values.
Results may differ from the reference program's by a relative error of at most 0.0052.
Values may be sent and summed in bfloat16 or wider, within the bound.
No kernel may reach another device: no remote copies, remote signals or barrier semaphores. Data moves between devices by JAX's collectives and lax.ppermute only.
A program may use at most 128 MiB of HBM per device.

```python
import jax
import jax.numpy as jnp
from jax import lax

D = 4096
H = 32
DH = 128
TOK_DEV = 1024
TOKENS = 8192


def block_levels(key, shape, cuts, least, high):
    level, own = 1.0, jax.random.fold_in(key, 6)
    for dim, parts in cuts:
        draws = jnp.exp(jax.random.uniform(jax.random.fold_in(own, dim), (parts,), jnp.float32, least / len(cuts), high / len(cuts)))
        level = level * jnp.repeat(draws, shape[dim] // parts).reshape([-1 if axis == dim else 1 for axis in range(len(shape))])
    return level


def centred(own_key, shape, deviation, bound, cuts=(), dtype=jnp.bfloat16):
    array = deviation * jax.random.normal(own_key, shape, jnp.float32)
    if cuts:
        array = array * block_levels(own_key, shape, cuts, -0.22, 0.18)
    return jnp.clip(array, -bound, bound).astype(dtype)


def setup_inputs(seed: int = 0, part: int = 0) -> dict:
    splits = jax.random.split(jax.random.key(seed), 6)
    part_splits = jax.random.split(jax.random.fold_in(splits[5], part), 6)
    queries = centred(part_splits[0], (TOKENS, H * DH), 1.0, 6.0, ((0, 8), (1, 2)))
    keys = centred(part_splits[1], (TOKENS, H * DH), 1.0, 6.0, ((0, 8), (1, 2)))
    values = centred(part_splits[2], (TOKENS, H * DH), 1.0, 6.0, ((0, 8), (1, 2)))
    out_weight = centred(splits[3], (H * DH, D), (H * DH) ** -0.5, 0.09375, ((0, 2), (1, 8)))
    norm_gain = jnp.clip(1.0 + 0.18 * jax.random.normal(splits[4], (H * DH,), jnp.float32), 0.1, 1.9)
    return dict(queries=queries, keys=keys, values=values, out_weight=out_weight, norm_gain=norm_gain)


def block_out(items):
    query_blk, key_blk, value_blk, prefix = items
    query_f = query_blk.astype(jnp.float32)
    scores = jnp.einsum('qhd,khd->hqk', query_f, key_blk.astype(jnp.float32))
    row_ids = lax.broadcasted_iota(jnp.int32, (TOK_DEV, TOK_DEV), 0)
    col_ids = lax.broadcasted_iota(jnp.int32, (TOK_DEV, TOK_DEV), 1)
    causal = (col_ids <= row_ids)[None, :, :]
    weights = jnp.where(causal, scores, 0.0).astype(jnp.bfloat16)
    intra = jnp.einsum('hqk,khd->qhd', weights.astype(jnp.float32), value_blk.astype(jnp.float32))
    inter = jnp.einsum('qhd,hde->qhe', query_f, prefix, precision=lax.Precision.HIGHEST)
    return intra + inter

def reference(queries, keys, values, out_weight, norm_gain):
    blocks = TOKENS // TOK_DEV
    query_all = queries.reshape(blocks, TOK_DEV, H, DH)
    key_all = keys.reshape(blocks, TOK_DEV, H, DH)
    value_all = values.reshape(blocks, TOK_DEV, H, DH)
    local_state = jnp.einsum('bkhd,bkhe->bhde', key_all.astype(jnp.float32), value_all.astype(jnp.float32))
    running = jnp.cumsum(local_state, axis=0)
    prefix_state = jnp.concatenate([jnp.zeros((1, H, DH, DH), jnp.float32), running[:-1]], axis=0)
    mixed = lax.map(block_out, (query_all, key_all, value_all, prefix_state))
    mean_sq = lax.optimization_barrier(jnp.mean(mixed * mixed, axis=-1, keepdims=True))
    gain = norm_gain.reshape(H, DH)
    normed = (mixed * lax.rsqrt(mean_sq + 1e-06) * gain).astype(jnp.bfloat16)
    normed = normed.reshape(TOKENS, H * DH)
    return jnp.dot(normed, out_weight, preferred_element_type=jnp.float32).astype(jnp.bfloat16)
```

```python
import functools

import jax
import jax.numpy as jnp
from jax import lax
from jax.experimental import pallas as pl
from jax.experimental.pallas import tpu as pltpu
from jax.sharding import PartitionSpec as P

DH = 128
LANES = 128
EPS = 1e-06
F32 = jnp.float32
BF16 = jnp.bfloat16
MIB = 1 << 20


def params(mib=32):
    return pltpu.CompilerParams(vmem_limit_bytes=mib * MIB)


def dot(a, b):
    return lax.dot_general(a, b, (((1,), (0,)), ((), ())), preferred_element_type=F32)


def dot_nt(a, b):
    return lax.dot_general(a, b, (((1,), (1,)), ((), ())), preferred_element_type=F32)


def dot_tn(a, b):
    return lax.dot_general(a, b, (((0,), (0,)), ((), ())), preferred_element_type=F32)


def state_kernel(per, k_ref, v_ref, out_ref):
    for i in range(per):
        cols = slice(i * DH, (i + 1) * DH)
        out_ref[i] = dot_tn(k_ref[:, cols], v_ref[:, cols]).astype(BF16)


def block_states(keys, values, heads):
    rows = keys.shape[0]
    per = 4 if heads % 4 == 0 else 1
    spec = pl.BlockSpec((rows, per * DH), lambda i: (0, i))
    return pl.pallas_call(
        functools.partial(state_kernel, per),
        grid=(heads // per,),
        in_specs=[spec, spec],
        out_specs=pl.BlockSpec((per, DH, DH), lambda i: (i, 0, 0)),
        out_shape=jax.ShapeDtypeStruct((heads, DH, DH), BF16),
        compiler_params=params(),
        cost_estimate=pl.CostEstimate(
            flops=8 * rows * heads * DH * DH, bytes_accessed=4 * keys.size, transcendentals=0
        ),
        name="block_states",
    )(keys, values)


def intra_kernel(per, chunk, q_ref, k_ref, v_ref, out_ref):
    rows = q_ref.shape[0]
    row_ids = lax.broadcasted_iota(jnp.int32, (chunk, chunk), 0)
    col_ids = lax.broadcasted_iota(jnp.int32, (chunk, chunk), 1)
    causal = col_ids <= row_ids
    for i in range(per):
        cols = slice(i * DH, (i + 1) * DH)
        state = None
        for at in range(0, rows, chunk):
            part = slice(at, at + chunk)
            q, k, v = q_ref[part, cols], k_ref[part, cols], v_ref[part, cols]
            scores = jnp.where(causal, dot_nt(q, k), 0.0).astype(BF16)
            mixed = dot(scores, v)
            if state is not None:
                mixed = mixed + dot(q, state.astype(BF16))
            out_ref[part, cols] = mixed
            if at + chunk < rows:
                step = dot_tn(k, v)
                state = step if state is None else state + step


def intra_block(queries, keys, values, heads):
    rows = queries.shape[0]
    per = 2 if heads % 2 == 0 else 1
    chunk = 256 if rows % 256 == 0 else rows
    spec = pl.BlockSpec((rows, per * DH), lambda i: (0, i))
    return pl.pallas_call(
        functools.partial(intra_kernel, per, chunk),
        grid=(heads // per,),
        in_specs=[spec, spec, spec],
        out_specs=spec,
        out_shape=jax.ShapeDtypeStruct(queries.shape, F32),
        compiler_params=params(),
        cost_estimate=pl.CostEstimate(
            flops=16 * rows * heads * DH * DH, bytes_accessed=10 * queries.size, transcendentals=0
        ),
        name="intra_block",
    )(queries, keys, values)


def norm_kernel(n_sib, table, q_ref, a_ref, p_ref, g_ref, *refs):
    sib_refs, out_ref = refs[:n_sib], refs[-1]
    state = p_ref[0].astype(F32)
    for o in range(n_sib):
        state = state + jnp.where(table[2 + o] > 0, sib_refs[o][0].astype(F32), 0.0)
    mixed = a_ref[...] + dot(q_ref[...], state.astype(BF16))
    mean_sq = jnp.mean(mixed * mixed, axis=-1, keepdims=True)
    out_ref[...] = (mixed * lax.rsqrt(mean_sq + EPS) * g_ref[0]).astype(BF16)


def norm_part(table, queries, intra, prefix, gain, sibs, normed):
    rows, width = queries.shape
    part = prefix.shape[0]
    cols = pl.BlockSpec((rows, DH), lambda i, t: (0, t[0] * part + i))
    mat = pl.BlockSpec((1, DH, DH), lambda i, t: (t[0] * part + i, 0, 0))
    in_specs = [
        cols,
        cols,
        pl.BlockSpec((1, DH, DH), lambda i, t: (i, 0, 0)),
        pl.BlockSpec((1, 1, DH), lambda i, t: (t[0] * part + i, 0, 0)),
    ] + [mat] * len(sibs)
    operands = [queries, intra, prefix, gain, *sibs]
    aliases = {}
    if normed is not None:
        in_specs.append(pl.BlockSpec(memory_space=pl.ANY))
        operands.append(normed)
        aliases = {len(operands): 0}
    return pl.pallas_call(
        functools.partial(norm_kernel, len(sibs)),
        grid_spec=pltpu.PrefetchScalarGridSpec(
            num_scalar_prefetch=1, grid=(part,), in_specs=in_specs, out_specs=cols
        ),
        out_shape=jax.ShapeDtypeStruct((rows, width), BF16),
        input_output_aliases=aliases,
        compiler_params=params(),
        cost_estimate=pl.CostEstimate(
            flops=4 * rows * part * DH * DH, bytes_accessed=8 * rows * part * DH, transcendentals=0
        ),
        name="norm_part",
    )(table, *operands)


def project_kernel(n_head, n_sub, table, x_ref, *refs):
    w_refs, outs = refs[: n_head * n_sub], refs[n_head * n_sub :]
    own = table[0]
    for kh in range(n_head):
        for j in range(n_sub):
            res = dot(x_ref[...], w_refs[kh * n_sub + j][...])
            at = slice(j * LANES, (j + 1) * LANES)
            for o in range(n_head):

                @pl.when(jnp.bitwise_xor(own, kh) == o)
                def _(res=res, at=at, o=o):
                    outs[o][:, at] = res.astype(outs[o].dtype)


def project(table, normed, pieces, n_head, n_sub):
    rows, depth = normed.shape
    tile = 256 if rows % 256 == 0 else rows
    width = n_sub * LANES
    out_spec = pl.BlockSpec((tile, width), lambda i, t: (i, 0))
    return pl.pallas_call(
        functools.partial(project_kernel, n_head, n_sub),
        grid_spec=pltpu.PrefetchScalarGridSpec(
            num_scalar_prefetch=1,
            grid=(rows // tile,),
            in_specs=[pl.BlockSpec((tile, depth), lambda i, t: (i, 0))]
            + [pl.BlockSpec((depth, LANES), lambda i, t: (0, 0))] * len(pieces),
            out_specs=[out_spec] * n_head,
        ),
        out_shape=[jax.ShapeDtypeStruct((rows, width), F32)]
        + [jax.ShapeDtypeStruct((rows, width), BF16)] * (n_head - 1),
        compiler_params=params(),
        cost_estimate=pl.CostEstimate(
            flops=2 * rows * depth * width * n_head,
            bytes_accessed=2 * rows * depth + 2 * depth * width * n_head + 6 * rows * width,
            transcendentals=0,
        ),
        name="project",
    )(table, normed, *pieces)


def combine_kernel(n_recv, table, keep_ref, *refs):
    total = keep_ref[...]
    for r in refs[:n_recv]:
        total = total + r[...].astype(F32)
    refs[-1][...] = total.astype(BF16)


def combine(table, keep, recvs, out, shape):
    rows = shape[0]
    n_sub = keep.shape[1] // LANES
    block = pl.BlockSpec((rows, LANES), lambda i, t: (0, i))
    in_specs = [block] * (1 + len(recvs))
    operands = [keep, *recvs]
    aliases = {}
    if out is not None:
        in_specs.append(pl.BlockSpec(memory_space=pl.ANY))
        operands.append(out)
        aliases = {len(operands): 0}
    return pl.pallas_call(
        functools.partial(combine_kernel, len(recvs)),
        grid_spec=pltpu.PrefetchScalarGridSpec(
            num_scalar_prefetch=1,
            grid=(n_sub,),
            in_specs=in_specs,
            out_specs=pl.BlockSpec((rows, LANES), lambda i, t: (0, t[i])),
        ),
        out_shape=jax.ShapeDtypeStruct(shape, BF16),
        input_output_aliases=aliases,
        compiler_params=params(),
        cost_estimate=pl.CostEstimate(
            flops=2 * keep.size, bytes_accessed=8 * keep.size, transcendentals=0
        ),
        name="combine",
    )(table, *operands)


def shift(x, axis, size, o):
    return lax.ppermute(x, axis, [(i, (i + o) % size) for i in range(size)])


def swap(x, axis, size, k):
    return lax.ppermute(x, axis, [(i, i ^ k) for i in range(size)])


def table(*entries):
    return jnp.stack([jnp.asarray(e, jnp.int32) for e in entries])


def local(sizes, queries, keys, values, out_weight, norm_gain):
    n_group, n_ctx, n_head, n_sub = (sizes[a] for a in ("groups", "ctx", "head", "sub"))
    g, c, h, s = (lax.axis_index(a) for a in ("groups", "ctx", "head", "sub"))
    rows, width = queries.shape
    heads = width // DH
    depth, cols = out_weight.shape
    near = n_ctx // n_head
    split = n_group if cols % (n_group * LANES) == 0 else 1
    rounds = cols // (split * LANES)
    low, own = c % near, (c // near) ^ h

    def mine(o, r):
        return ((g - o) % split) * rounds + r

    def cut(o, r):
        return lax.dynamic_slice(out_weight, (0, mine(o, r) * LANES), (depth, LANES))

    first = {(o, r): cut(o, r) for o in range(split) for r in range(rounds)}
    pieces = {}

    def fetch(r, k):
        for o in range(split):
            if k == 0:
                piece = first[o, r]
            elif o == 0:
                piece = swap(first[0, r], "ctx", n_ctx, k)
            else:
                piece = shift(pieces[r, k, 0][0], "groups", n_group, o)
            pieces[r, k, o] = [piece] + [shift(piece, "sub", n_sub, j) for j in range(1, n_sub)]

    part = heads // n_sub
    states = block_states(keys, values, heads)
    sibs = [shift(states, "sub", n_sub, o) for o in range(1, n_sub)]
    total = sum(
        lax.dynamic_slice_in_dim(x, s * part, part).astype(F32) for x in [states, *sibs]
    )
    prefix = jnp.zeros((part, DH, DH), BF16)
    for i in range(n_ctx - 1):
        prefix = prefix + lax.ppermute(
            (prefix.astype(F32) + total).astype(BF16), "ctx", [(i, i + 1)]
        )
    intra = intra_block(queries, keys, values, heads)
    gain = norm_gain.reshape(heads, 1, DH)
    normed = None
    for o in range(n_sub):
        mat = prefix if o == 0 else shift(prefix, "sub", n_sub, o)
        at = table((s - o) % n_sub, 0, *[s >= j for j in range(1, n_sub)])
        normed = norm_part(at, queries, intra, mat, gain, sibs, normed)

    for r in range(rounds):
        for kl in range(near):
            for kh in range(n_head):
                fetch(r, kh * near + kl)
    out = None
    for r in range(rounds):
        for kl in range(near):
            for o in range(split):
                use = [p for kh in range(n_head) for p in pieces[r, kh * near + kl, o]]
                keep, *sends = project(table(own), normed, use, n_head, n_sub)
                recvs = [swap(x, "head", n_head, i + 1) for i, x in enumerate(sends)]
                places = [
                    (((low ^ kl) * n_sub + (s - j) % n_sub) * split * rounds + mine(o, r))
                    for j in range(n_sub)
                ]
                out = combine(table(*places), keep, recvs, out, (rows, n_sub * near * cols))
    return out


def solution(mesh):
    return jax.shard_map(
        functools.partial(local, dict(mesh.shape)),
        mesh=mesh,
        in_specs=(
            P(("groups", "ctx", "sub"), "head"),
            P(("groups", "ctx", "sub"), "head"),
            P(("groups", "ctx", "sub"), "head"),
            P("head", ("ctx", "sub")),
            P("head"),
        ),
        out_specs=P(("groups", "ctx", "sub"), "head"),
        check_vma=False,
    )
```

```python
import functools

import jax
import jax.numpy as jnp
from jax import lax
from jax.experimental import pallas as pl
from jax.experimental.pallas import tpu as pltpu
from jax.sharding import PartitionSpec as P

DH = 128
LANES = 128
EPS = 1e-06
F32 = jnp.float32
BF16 = jnp.bfloat16
MIB = 1 << 20
VMEM_MIB = 16
ATTN_MIB = 16
ANY = pl.BlockSpec(memory_space=pl.ANY)
HBM = pl.BlockSpec(memory_space=pltpu.HBM)


def params(mib=VMEM_MIB):
    return pltpu.CompilerParams(vmem_limit_bytes=mib * MIB)


def dot(a, b):
    return lax.dot_general(a, b, (((1,), (0,)), ((), ())), preferred_element_type=F32)


def cost(us):
    return pl.CostEstimate(flops=int(us * 1e9), bytes_accessed=int(us * 3e6), transcendentals=0)


def dot_nt(a, b):
    return lax.dot_general(a, b, (((1,), (1,)), ((), ())), preferred_element_type=F32)


def dot_tn(a, b):
    return lax.dot_general(a, b, (((0,), (0,)), ((), ())), preferred_element_type=F32)


def gate_kernel(*refs):
    pass


def gate(x, *deps):
    return pl.pallas_call(
        gate_kernel,
        in_specs=[ANY] * (1 + len(deps)),
        out_specs=ANY,
        out_shape=jax.ShapeDtypeStruct(x.shape, x.dtype),
        input_output_aliases={0: 0},
        compiler_params=params(),
        cost_estimate=cost(0.01),
        name="gate",
    )(x, *deps)


def pair_up(mats):
    zero = jnp.zeros_like(mats[0])
    return jnp.concatenate(
        [
            jnp.concatenate([m if i == j else zero for j in range(len(mats))], axis=1)
            for i, m in enumerate(mats)
        ],
        axis=0,
    )


def split_dot(a, b):
    high = b.astype(BF16)
    return dot(a, high) + dot(a, (b - high.astype(F32)).astype(BF16))


def heads_of(i, size):
    return slice(i * DH, (i + size) * DH)


def state_kernel(per, size, steps, k_hbm, v_hbm, *refs):
    out_hbm, send_hbm = refs[-2:]

    def body(k_ref, v_ref, out_ref, send_ref):
        for i in range(0, per, size):
            state = dot_tn(k_ref[:, heads_of(i, size)], v_ref[:, heads_of(i, size)])
            for j in range(size):
                own = state[heads_of(j, 1), heads_of(j, 1)]
                out_ref[i + j] = own
                send_ref[i + j] = own.astype(BF16)

    spec = pl.BlockSpec((k_hbm.shape[0], per * DH), lambda i: (0, i))
    state = pl.BlockSpec((per, DH, DH), lambda i: (i, 0, 0))
    pltpu.emit_pipeline(body, grid=(steps,), in_specs=[spec] * 2, out_specs=[state] * 2)(
        k_hbm, v_hbm, out_hbm, send_hbm
    )


def block_states(keys, values, heads, *deps):
    per = 4 if heads % 4 == 0 else 1
    size = 2 if per % 2 == 0 else 1
    return pl.pallas_call(
        functools.partial(state_kernel, per, size, heads // per),
        in_specs=[HBM] * 2 + [ANY] * len(deps),
        out_specs=[ANY] * 2,
        out_shape=[jax.ShapeDtypeStruct((heads, DH, DH), t) for t in (F32, BF16)],
        compiler_params=params(60),
        cost_estimate=cost(1000),
        name="block_states",
    )(keys, values, *deps)


def intra_kernel(size, chunk, steps, first, place, q_hbm, k_hbm, v_hbm, *refs):
    rows = q_hbm.shape[0]
    row_ids = lax.broadcasted_iota(jnp.int32, (chunk, chunk), 0)
    col_ids = lax.broadcasted_iota(jnp.int32, (chunk, chunk), 1)
    causal = col_ids <= row_ids

    def body(q_ref, k_ref, v_ref, out_ref):
        state = None
        for at in range(0, rows, chunk):
            part = slice(at, at + chunk)
            for i in range(size):
                cols = heads_of(i, 1)
                scores = dot_nt(q_ref[part, cols], k_ref[part, cols])
                scores = jnp.where(causal, scores, 0.0).astype(BF16)
                mixed = dot(scores, v_ref[part, cols])
                if state is not None:
                    mixed = mixed + split_dot(q_ref[part, cols], state[i])
                out_ref[part, cols] = mixed
            if at + chunk < rows:
                step = dot_tn(k_ref[part, :], v_ref[part, :])
                step = [step[heads_of(i, 1), heads_of(i, 1)] for i in range(size)]
                state = step if state is None else [a + b for a, b in zip(state, step)]

    start = first(place)
    spec = pl.BlockSpec((rows, size * DH), lambda i: (0, start + i))
    out = pl.BlockSpec((rows, size * DH), lambda i: (0, i))
    pltpu.emit_pipeline(body, grid=(steps,), in_specs=[spec] * 3, out_specs=[out])(
        q_hbm, k_hbm, v_hbm, refs[-2]
    )
    refs[-1][...] = jnp.zeros_like(refs[-1])


def intra_block(place, o, b, n_sub, n_band, queries, keys, values, part, *deps):
    rows = queries.shape[0]
    part //= n_band
    size = 2 if part % 2 == 0 else 1
    steps = part // size
    chunk = 256 if rows % 256 == 0 else rows

    def first(t):
        return (lax.rem(t[3] + (n_sub - o), n_sub) * n_band + b) * steps

    return pl.pallas_call(
        functools.partial(intra_kernel, size, chunk, steps, first),
        grid_spec=pltpu.PrefetchScalarGridSpec(
            num_scalar_prefetch=1,
            grid=(1,),
            in_specs=[HBM] * 3 + [ANY] * len(deps),
            out_specs=[ANY, pl.BlockSpec((8, LANES), lambda i, t: (0, 0))],
        ),
        out_shape=[
            jax.ShapeDtypeStruct((rows, part * DH), F32),
            jax.ShapeDtypeStruct((8, LANES), F32),
        ],
        compiler_params=params(40),
        cost_estimate=cost(4.4),
        name="intra_block",
    )(place, queries, keys, values, *deps)


def norm_kernel(per, size, n_sub, o, place, q_ref, a_ref, p_ref, g_ref, *refs):
    sib_refs, out_ref = refs[: n_sub - 1], refs[-2]
    refs[-1][...] = jnp.zeros_like(refs[-1])
    for i in range(0, per, size):
        mats = []
        for j in range(i, i + size):
            state = p_ref[j].astype(F32)
            for n, sib in enumerate(sib_refs):
                state = state + jnp.where(place[3] >= n + 1, sib[j].astype(F32), 0.0)
            mats.append(state)
        both = a_ref[:, heads_of(i, size)] + split_dot(q_ref[:, heads_of(i, size)], pair_up(mats))
        for j in range(size):
            mixed = both[:, heads_of(j, 1)]
            mean_sq = jnp.mean(mixed * mixed, axis=-1, keepdims=True)
            normed = mixed * lax.rsqrt(mean_sq + EPS) * g_ref[i + j]
            out_ref[:, heads_of(i + j, 1)] = normed.astype(BF16)


def norm_part(place, o, b, n_sub, n_band, queries, intra, prefix, gain, sibs, normed, *deps):
    rows, width = queries.shape
    part = prefix.shape[0] // n_band
    per = 4 if part % 4 == 0 else 1
    size = 2 if per % 2 == 0 else 1
    steps = part // per

    def which(t):
        return (lax.rem(t[3] - o + n_sub, n_sub) * n_band + b) * steps

    cols = pl.BlockSpec((rows, per * DH), lambda i, t: (0, which(t) + i))
    mat = pl.BlockSpec((per, DH, DH), lambda i, t: (which(t) + i, 0, 0))
    in_specs = [
        cols,
        pl.BlockSpec((rows, per * DH), lambda i, t: (0, i)),
        pl.BlockSpec((per, DH, DH), lambda i, t: (b * steps + i, 0, 0)),
        pl.BlockSpec((per, 1, DH), lambda i, t: (which(t) + i, 0, 0)),
    ] + [mat] * len(sibs)
    operands = [queries, intra, prefix, gain, *sibs, *deps]
    in_specs += [ANY] * len(deps)
    aliases = {}
    if normed is not None:
        in_specs.append(ANY)
        operands.append(normed)
        aliases = {len(operands): 0}
    return pl.pallas_call(
        functools.partial(norm_kernel, per, size, n_sub, o),
        grid_spec=pltpu.PrefetchScalarGridSpec(
            num_scalar_prefetch=1,
            grid=(steps,),
            in_specs=in_specs,
            out_specs=[cols, pl.BlockSpec((8, LANES), lambda i, t: (0, 0))],
        ),
        out_shape=[
            jax.ShapeDtypeStruct((rows, width), BF16),
            jax.ShapeDtypeStruct((8, LANES), F32),
        ],
        input_output_aliases=aliases,
        compiler_params=params(ATTN_MIB),
        cost_estimate=cost(1.8),
        name="norm_part",
    )(place, *operands)


class Plan:
    def __init__(self, sizes, cols):
        self.n_group, self.n_ctx, self.n_head, self.n_sub = (
            sizes[a] for a in ("groups", "ctx", "head", "sub")
        )
        self.near = self.n_ctx // self.n_head
        self.split = self.n_group if cols % (self.n_group * LANES) == 0 else 1
        self.rounds = cols // (self.split * LANES)
        self.tiles = self.split * self.rounds
        self.line = self.n_head == 2 and self.near == 2

    def own(self, place):
        return jnp.bitwise_xor(place[1] // self.near, place[2])

    def mine(self, place, step):
        r, _, o, _ = step
        return lax.rem(place[0] + (self.n_group - o), self.split) * self.rounds + r

    def target(self, place, step, j):
        low = jnp.bitwise_xor(lax.rem(place[1], self.near), step[1])
        if self.line:
            far = jnp.where(place[1] < self.near, step[1], self.near - 1 - step[1])
            low = jnp.where(self.own(place) == 0, low, far)
        sub = lax.rem(place[3] + (self.n_sub - j), self.n_sub)
        return (low * self.n_sub + sub) * self.tiles + self.mine(place, step)

    def holder(self, place, step, kh, j):
        low = jnp.bitwise_xor(lax.rem(place[1], self.near), step[1])
        far = jnp.where(place[1] < self.near, step[1], self.near - 1 - step[1])
        half = place[1] // self.near
        ctx = half * self.near + low if kh == 0 else (1 - half) * self.near + far
        group = lax.rem(place[0] + (self.n_group - step[2]), self.split)
        sub = lax.rem(place[3] + (self.n_sub - j), self.n_sub)
        return (group * self.n_ctx + ctx) * self.n_sub + sub


def lanes(i, count):
    return pl.ds(pl.multiple_of(i * LANES, LANES), count * LANES)


def add_up(plan, step, place, stage, keep_hbm, recv_hbm, out_hbm, sems):
    keep, recv, total = stage
    ins = [pltpu.make_async_copy(keep_hbm, keep, sems.at[0])]
    ins += [
        pltpu.make_async_copy(r, recv.at[i], sems.at[1 + i]) for i, r in enumerate(recv_hbm)
    ]
    outs = [
        pltpu.make_async_copy(
            total.at[:, j * step[3] * LANES : (j + 1) * step[3] * LANES],
            out_hbm.at[:, lanes(plan.target(place, step, j), step[3])],
            sems.at[plan.n_head + j],
        )
        for j in range(plan.n_sub)
    ]

    def middle():
        for copy in ins:
            copy.wait()
        value = keep[...]
        for i in range(len(recv_hbm)):
            value = value + recv[i].astype(F32)
        total[...] = value.astype(BF16)
        for copy in outs:
            copy.start()

    def last():
        for copy in outs:
            copy.wait()

    for copy in ins:
        copy.start()
    return middle, last


def project_kernel(plan, step, which, kinds, before, n_deps, place, x_hbm, *refs):
    n_head, n_sub = plan.n_head, plan.n_sub
    refs = list(refs)

    def take(n):
        got = refs[:n]
        del refs[:n]
        return got

    w_hbm = take(len(kinds))
    if before is not None:
        keep_old, recv_old = take(1)[0], take(n_head - 1)
    take(n_deps)
    if before is not None:
        take(1 if before[1] else 0)
    res_hbm = take(len(which))
    if before is not None:
        out_hbm = take(1)[0]
    x, w, keep, send, old_keep, old_recv, total, x_sem, w_sem, res_sem, old_sem = refs
    rows = x.shape[0]
    tiles = [slice(j * step[3] * LANES, (j + 1) * step[3] * LANES) for j in range(n_sub)]
    tile = 256 if rows % 256 == 0 else rows
    own = plan.own(place)
    loads = []
    for i in range(n_head * n_sub):
        if kinds[0] == 3:
            src = w_hbm[0].at[plan.holder(place, step, i // n_sub, i % n_sub)]
        else:
            src = w_hbm[i]
            if kinds[i]:
                src = src.at[:, lanes(plan.mine(place, step), step[3])]
        dst = w.at[i // n_sub, :, tiles[i % n_sub]]
        loads.append(pltpu.make_async_copy(src, dst, w_sem.at[i]))
    parts = [slice(at, at + tile) for at in range(0, rows, tile)]
    rows_in = [
        pltpu.make_async_copy(x_hbm.at[p], x.at[p], x_sem.at[i]) for i, p in enumerate(parts)
    ]
    rows_in[0].start()
    for copy in loads:
        copy.start()
    for copy in rows_in[1:]:
        copy.start()
    if before is not None:
        stage = (old_keep, old_recv, total)
        middle, last = add_up(
            plan, before[0], place, stage, keep_old, recv_old, out_hbm, old_sem
        )
    results = []
    for n, o in enumerate(which):
        slot = jnp.bitwise_xor(own, o)
        for j in range(n_sub):
            dst = w.at[slot, :, tiles[j]]
            pltpu.make_async_copy(dst, dst, w_sem.at[slot * n_sub + j]).wait()
        for i, p in enumerate(parts):
            if n == 0:
                rows_in[i].wait()
            res = dot(x[p], w[slot])
            if o == 0:
                keep[p] = res
            else:
                send[o - 1, p] = res.astype(BF16)
        src = keep if o == 0 else send.at[o - 1]
        results.append(pltpu.make_async_copy(src, res_hbm[n], res_sem.at[o]))
        results[-1].start()
        if before is not None and n == 0:
            middle()
    for o in range(n_head):
        if o not in which:
            slot = jnp.bitwise_xor(own, o)
            for j in range(n_sub):
                dst = w.at[slot, :, tiles[j]]
                pltpu.make_async_copy(dst, dst, w_sem.at[slot * n_sub + j]).wait()
    for copy in results:
        copy.wait()
    if before is not None:
        last()


def project(plan, place, step, which, normed, pieces, before, out, deps):
    rows, depth = normed.shape
    n_head, n_sub = plan.n_head, plan.n_sub
    width = n_sub * step[3] * LANES
    kinds = [3 if p.ndim == 3 else int(p.shape[1] != step[3] * LANES) for p in pieces]
    operands = [normed, *pieces]
    shapes = [jax.ShapeDtypeStruct((rows, width), BF16 if o else F32) for o in which]
    aliases, info = {}, None
    if before is not None:
        operands += [before[1], *before[2]]
        info = (before[0], out is not None)
    operands += deps
    if before is not None:
        shapes.append(jax.ShapeDtypeStruct((rows, n_sub * plan.near * plan.tiles * LANES), BF16))
        if out is not None:
            operands.append(out)
            aliases = {len(operands): len(shapes) - 1}
    tiles = rows // 256 if rows % 256 == 0 else 1
    old = width if before is None else n_sub * before[0][3] * LANES
    dma = pltpu.SemaphoreType.DMA
    return pl.pallas_call(
        functools.partial(project_kernel, plan, step, which, kinds, info, len(deps)),
        grid_spec=pltpu.PrefetchScalarGridSpec(
            num_scalar_prefetch=1,
            grid=(1,),
            in_specs=[ANY] * len(operands),
            out_specs=[ANY] * len(shapes),
            scratch_shapes=[
                pltpu.VMEM((rows, depth), BF16),
                pltpu.VMEM((n_head, depth, width), BF16),
                pltpu.VMEM((rows, width), F32),
                pltpu.VMEM((max(1, n_head - 1), rows, width), BF16),
                pltpu.VMEM((rows, old), F32),
                pltpu.VMEM((max(1, n_head - 1), rows, old), BF16),
                pltpu.VMEM((rows, old), BF16),
                dma((tiles,)),
                dma((n_head * n_sub,)),
                dma((n_head,)),
                dma((n_head + n_sub,)),
            ],
        ),
        out_shape=shapes,
        input_output_aliases=aliases,
        compiler_params=params(32),
        cost_estimate=cost(2.7),
        name="project",
    )(place, *operands)


def combine_kernel(plan, step, n_recv, place, *refs):
    keep_hbm, recv_hbm = refs[0], refs[1 : 1 + n_recv]
    out_hbm, keep, recv, total, sems = refs[-5:]
    middle, last = add_up(
        plan, step, place, (keep, recv, total), keep_hbm, recv_hbm, out_hbm, sems
    )
    middle()
    last()


def combine(plan, place, step, keep, recvs, out):
    rows, width = keep.shape
    operands = [keep, *recvs, out]
    return pl.pallas_call(
        functools.partial(combine_kernel, plan, step, len(recvs)),
        grid_spec=pltpu.PrefetchScalarGridSpec(
            num_scalar_prefetch=1,
            grid=(1,),
            in_specs=[ANY] * len(operands),
            out_specs=ANY,
            scratch_shapes=[
                pltpu.VMEM((rows, width), F32),
                pltpu.VMEM((max(1, len(recvs)), rows, width), BF16),
                pltpu.VMEM((rows, width), BF16),
                pltpu.SemaphoreType.DMA((plan.n_head + plan.n_sub,)),
            ],
        ),
        out_shape=jax.ShapeDtypeStruct(out.shape, BF16),
        input_output_aliases={len(operands): 0},
        compiler_params=params(),
        cost_estimate=cost(0.5),
        name="combine",
    )(place, *operands)


def shift(x, axis, size, o):
    return lax.ppermute(x, axis, [(i, (i + o) % size) for i in range(size)])


def swap(x, axis, size, k):
    return lax.ppermute(x, axis, [(i, i ^ k) for i in range(size)])


def local(sizes, queries, keys, values, out_weight, norm_gain):
    rows, width = queries.shape
    heads = width // DH
    depth, cols = out_weight.shape
    plan = Plan(sizes, cols)
    n_group, n_ctx, n_head, n_sub = plan.n_group, plan.n_ctx, plan.n_head, plan.n_sub
    near, split, rounds = plan.near, plan.split, plan.rounds
    place = jnp.stack([lax.axis_index(a) for a in ("groups", "ctx", "head", "sub")]).astype(jnp.int32)
    s = place[3]

    steps = [(r, kl, o, 1) for r in range(rounds) for kl in range(near) for o in range(split)]
    line = plan.line and rounds == 2 and split == 2

    whole = [out_weight] + [shift(out_weight, "sub", n_sub, j) for j in range(1, n_sub)]

    def cut(r, count):
        at = plan.mine(place, (r, 0, 0, count)) * LANES
        return lax.dynamic_slice(out_weight, (0, at), (depth, count * LANES))

    first = [cut(r, 1) for r in range(rounds)]
    pieces = {(r, 0, o, 1, 0): whole for r in range(rounds) for o in range(split)}
    later = {}
    held = {step: [] for step in steps}

    def cross(piece):
        return [piece] + [shift(piece, "sub", n_sub, j) for j in range(1, n_sub)]

    def hold(n, *arrays):
        held[steps[n]] += arrays

    part = heads // n_sub
    states, sent = block_states(keys, values, heads, first[0])
    sibs = [shift(sent, "sub", n_sub, o) for o in range(1, n_sub)]
    total = sum(
        lax.dynamic_slice_in_dim(x, s * part, part).astype(F32) for x in [states, *sibs]
    )
    ends, middle, out_way = [(0, 1), (1, 0), (2, 3), (3, 2)], [(1, 2), (2, 1)], [(1, 0), (2, 3)]
    prefix = jnp.zeros((part, DH, DH), BF16)
    n_band = 1
    bands = [(o, b) for o in range(n_sub) for b in range(n_band)]
    intra, tokens, hops = {}, [], []
    for i in range(n_ctx - 1):
        hop = (prefix.astype(F32) + total).astype(BF16)
        if i:
            hop = gate(hop, *tokens[i - 1 : i])
        hops.append(hop)
        if i < len(bands):
            deps = [hop] if i == 0 else [hop, *whole[1:]]
            intra[bands[i]], token = intra_block(
                place, *bands[i], n_sub, n_band, queries, keys, values, part, *deps
            )
            tokens.append(token)
        prefix = prefix + lax.ppermute(hop, "ctx", [(i, i + 1)])
    gain = norm_gain.reshape(heads, 1, DH)

    normed, normed_token = None, None
    for o in range(n_sub):
        mat = prefix if o == 0 else shift(prefix, "sub", n_sub, o)
        for b in range(n_band):
            deps = []
            normed, token = norm_part(
                place, o, b, n_sub, n_band, queries, intra[o, b], mat, gain, sibs, normed, *deps
            )
            normed_token = token if normed_token is None else normed_token

    if line:
        inner = (place[1] == 1) | (place[1] == 2)

        def along(x, perm, *deps):
            return lax.ppermute(gate(x, *deps) if deps else x, "ctx", perm)

        def over(x, *deps):
            return shift(gate(x, *deps) if deps else x, "groups", n_group, 1)

        near_a = gate(along(first[0], ends), tokens[0])
        across_a = gate(along(first[0], middle), tokens[0])
        y_near_a = over(near_a)
        outward_a = gate(along(across_a, out_way), tokens[1])
        across_b = gate(along(near_a, middle), tokens[1])
        outward_b = gate(along(across_b, out_way), normed_token)
        far_a = jnp.where(inner, across_a, outward_a)
        far_b = jnp.where(inner, across_b, outward_b)
        across_c = along(first[1], middle, across_b)
        y_far_a = over(far_a, prefix)
        y_far_b = over(far_b, y_far_a, token)
        near_c = along(first[1], ends, outward_b)
        outward_c = along(across_c, out_way, normed_token)
        pieces[0, 0, 0, 1, 1] = cross(far_a)
        pieces[0, 0, 1, 1, 1] = cross(y_far_a)
        pieces[0, 1, 0, 1, 0] = cross(gate(near_a, prefix))
        pieces[0, 1, 0, 1, 1] = cross(far_b)
        pieces[0, 1, 1, 1, 0] = cross(gate(y_near_a, normed_token))
        hold(0, y_near_a, across_c, *pieces[0, 1, 0, 1, 0][1:])
        hold(1, near_c, outward_c, y_far_b, *pieces[0, 1, 0, 1, 1][1:], *pieces[0, 1, 1, 1, 0][1:])

        def after_0(*sent):
            pieces[0, 1, 1, 1, 1] = cross(gate(y_far_b, *sent))
            hold(2, *pieces[0, 1, 1, 1, 1][1:])

        def after_1(*sent):
            far_c = jnp.where(inner, across_c, gate(outward_c, *sent))
            pieces[1, 0, 0, 1, 1] = cross(far_c)
            later["y_far_c"] = over(far_c)
            later["across_d"] = along(near_c, middle, *sent)
            pieces[1, 1, 0, 1, 0] = cross(gate(near_c, *sent))
            hold(3, later["y_far_c"], later["across_d"], *pieces[1, 1, 0, 1, 0][1:])

        def after_2(*sent):
            outward_d = along(later["across_d"], out_way)
            later["y_near_c"] = over(near_c, later["y_far_c"])
            far_d = jnp.where(inner, later["across_d"], outward_d)
            pieces[1, 0, 1, 1, 1] = cross(later["y_far_c"])
            pieces[1, 1, 0, 1, 1] = cross(far_d)
            y_far_d = over(far_d, later["y_near_c"])
            hold(4, outward_d, later["y_near_c"])
            pieces[1, 1, 1, 1, 0] = cross(later["y_near_c"])
            pieces[1, 1, 1, 1, 1] = cross(y_far_d)
            hold(5, *pieces[1, 1, 0, 1, 1][1:])
            hold(6, y_far_d, *pieces[1, 1, 1, 1, 0][1:])

        later = {0: after_0, 1: after_1, 2: after_2}
    else:
        for r in range(rounds):
            for kl in range(near):
                for kh in range(n_head):
                    if kl or kh:
                        piece = swap(first[r], "ctx", n_ctx, kh * near + kl)
                        pieces[r, kl, 0, 1, kh] = cross(piece)
                        for o in range(1, split):
                            pieces[r, kl, o, 1, kh] = cross(shift(piece, "groups", n_group, o))

    out, sent, late = None, [], None
    waiting = []
    others = list(range(1, n_head))
    for n, step in enumerate(steps):
        use = [p for kh in range(n_head) for p in pieces[*step, kh]]
        before = waiting.pop(0) if len(waiting) > 1 else None
        which = others if n == 0 and len(steps) > 1 else others + [0]
        deps = held[step] + sent
        shares = list(project(plan, place, step, which, normed, use, before, out, deps))
        if before is not None:
            out = shares.pop()
        got = dict(zip(which, shares))
        sent = shares[:1]
        if late:
            waiting[0] = late(sent)
            late = None
        recvs = [swap(got[i], "head", n_head, i) for i in others]
        waiting.append((step, got.get(0), recvs))
        if n in later:
            later[n](*sent)
        if 0 not in got:

            def late(deps, step=step, use=use, recvs=recvs):
                return step, project(plan, place, step, [0], normed, use, None, None, deps)[0], recvs

    if out is None:
        out = jnp.zeros((rows, n_sub * near * cols), BF16)
    for step, keep, recvs in waiting:
        out = combine(plan, place, step, keep, recvs, out)
    return out


def solution(mesh):
    return jax.shard_map(
        functools.partial(local, dict(mesh.shape)),
        mesh=mesh,
        in_specs=(
            P(("groups", "ctx", "sub"), "head"),
            P(("groups", "ctx", "sub"), "head"),
            P(("groups", "ctx", "sub"), "head"),
            P("head", ("ctx", "sub")),
            P("head"),
        ),
        out_specs=P(("groups", "ctx", "sub"), "head"),
        check_vma=False,
    )
```

```python
import functools

import jax
import jax.numpy as jnp
from jax import lax
from jax.experimental import pallas as pl
from jax.experimental.pallas import tpu as pltpu
from jax.sharding import PartitionSpec as P

DH = 128
LANES = 128
EPS = 1e-06
F32 = jnp.float32
BF16 = jnp.bfloat16
MIB = 1 << 20
VMEM_MIB = 16
ATTN_MIB = 16
ANY = pl.BlockSpec(memory_space=pl.ANY)
HBM = pl.BlockSpec(memory_space=pltpu.HBM)


def params(mib=VMEM_MIB):
    return pltpu.CompilerParams(vmem_limit_bytes=mib * MIB)


def dot(a, b):
    return lax.dot_general(a, b, (((1,), (0,)), ((), ())), preferred_element_type=F32)


def cost(us):
    return pl.CostEstimate(flops=int(us * 1e9), bytes_accessed=int(us * 3e6), transcendentals=0)


def dot_nt(a, b):
    return lax.dot_general(a, b, (((1,), (1,)), ((), ())), preferred_element_type=F32)


def dot_tn(a, b):
    return lax.dot_general(a, b, (((0,), (0,)), ((), ())), preferred_element_type=F32)


def gate_kernel(*refs):
    pass


def gate(x, *deps):
    return pl.pallas_call(
        gate_kernel,
        in_specs=[ANY] * (1 + len(deps)),
        out_specs=ANY,
        out_shape=jax.ShapeDtypeStruct(x.shape, x.dtype),
        input_output_aliases={0: 0},
        compiler_params=params(),
        cost_estimate=cost(0.01),
        name="gate",
    )(x, *deps)


def pair_up(mats):
    zero = jnp.zeros_like(mats[0])
    return jnp.concatenate(
        [
            jnp.concatenate([m if i == j else zero for j in range(len(mats))], axis=1)
            for i, m in enumerate(mats)
        ],
        axis=0,
    )


def split_dot(a, b):
    high = b.astype(BF16)
    return dot(a, high) + dot(a, (b - high.astype(F32)).astype(BF16))


def heads_of(i, size):
    return slice(i * DH, (i + size) * DH)


def state_kernel(per, size, steps, k_hbm, v_hbm, *refs):
    out_hbm, send_hbm = refs[-2:]

    def body(k_ref, v_ref, out_ref, send_ref):
        for i in range(0, per, size):
            state = dot_tn(k_ref[:, heads_of(i, size)], v_ref[:, heads_of(i, size)])
            for j in range(size):
                own = state[heads_of(j, 1), heads_of(j, 1)]
                out_ref[i + j] = own
                send_ref[i + j] = own.astype(BF16)

    spec = pl.BlockSpec((k_hbm.shape[0], per * DH), lambda i: (0, i))
    state = pl.BlockSpec((per, DH, DH), lambda i: (i, 0, 0))
    pltpu.emit_pipeline(body, grid=(steps,), in_specs=[spec] * 2, out_specs=[state] * 2)(
        k_hbm, v_hbm, out_hbm, send_hbm
    )


def block_states(keys, values, heads, *deps):
    per = 4 if heads % 4 == 0 else 1
    size = 2 if per % 2 == 0 else 1
    return pl.pallas_call(
        functools.partial(state_kernel, per, size, heads // per),
        in_specs=[HBM] * 2 + [ANY] * len(deps),
        out_specs=[ANY] * 2,
        out_shape=[jax.ShapeDtypeStruct((heads, DH, DH), t) for t in (F32, BF16)],
        compiler_params=params(60),
        cost_estimate=cost(1000),
        name="block_states",
    )(keys, values, *deps)


def intra_kernel(size, chunk, steps, first, place, q_hbm, k_hbm, v_hbm, *refs):
    rows = q_hbm.shape[0]
    row_ids = lax.broadcasted_iota(jnp.int32, (chunk, chunk), 0)
    col_ids = lax.broadcasted_iota(jnp.int32, (chunk, chunk), 1)
    causal = col_ids <= row_ids

    def body(q_ref, k_ref, v_ref, out_ref):
        state = None
        for at in range(0, rows, chunk):
            part = slice(at, at + chunk)
            for i in range(size):
                cols = heads_of(i, 1)
                scores = dot_nt(q_ref[part, cols], k_ref[part, cols])
                scores = jnp.where(causal, scores, 0.0).astype(BF16)
                mixed = dot(scores, v_ref[part, cols])
                if state is not None:
                    mixed = mixed + split_dot(q_ref[part, cols], state[i])
                out_ref[part, cols] = mixed
            if at + chunk < rows:
                step = dot_tn(k_ref[part, :], v_ref[part, :])
                step = [step[heads_of(i, 1), heads_of(i, 1)] for i in range(size)]
                state = step if state is None else [a + b for a, b in zip(state, step)]

    start = first(place)
    spec = pl.BlockSpec((rows, size * DH), lambda i: (0, start + i))
    out = pl.BlockSpec((rows, size * DH), lambda i: (0, i))
    pltpu.emit_pipeline(body, grid=(steps,), in_specs=[spec] * 3, out_specs=[out])(
        q_hbm, k_hbm, v_hbm, refs[-2]
    )
    refs[-1][...] = jnp.zeros_like(refs[-1])


def intra_block(place, o, b, n_sub, n_band, queries, keys, values, part, *deps):
    rows = queries.shape[0]
    part //= n_band
    size = 2 if part % 2 == 0 else 1
    steps = part // size
    chunk = 256 if rows % 256 == 0 else rows

    def first(t):
        return (lax.rem(t[3] + (n_sub - o), n_sub) * n_band + b) * steps

    return pl.pallas_call(
        functools.partial(intra_kernel, size, chunk, steps, first),
        grid_spec=pltpu.PrefetchScalarGridSpec(
            num_scalar_prefetch=1,
            grid=(1,),
            in_specs=[HBM] * 3 + [ANY] * len(deps),
            out_specs=[ANY, pl.BlockSpec((8, LANES), lambda i, t: (0, 0))],
        ),
        out_shape=[
            jax.ShapeDtypeStruct((rows, part * DH), F32),
            jax.ShapeDtypeStruct((8, LANES), F32),
        ],
        compiler_params=params(46),
        cost_estimate=cost(4.4),
        name="intra_block",
    )(place, queries, keys, values, *deps)


def norm_kernel(per, size, n_sub, o, place, q_ref, a_ref, p_ref, g_ref, *refs):
    sib_refs, out_ref = refs[: n_sub - 1], refs[-2]
    refs[-1][...] = jnp.zeros_like(refs[-1])
    for i in range(0, per, size):
        mats = []
        for j in range(i, i + size):
            state = p_ref[j].astype(F32)
            for n, sib in enumerate(sib_refs):
                state = state + jnp.where(place[3] >= n + 1, sib[j].astype(F32), 0.0)
            mats.append(state)
        both = a_ref[:, heads_of(i, size)] + split_dot(q_ref[:, heads_of(i, size)], pair_up(mats))
        for j in range(size):
            mixed = both[:, heads_of(j, 1)]
            mean_sq = jnp.mean(mixed * mixed, axis=-1, keepdims=True)
            normed = mixed * lax.rsqrt(mean_sq + EPS) * g_ref[i + j]
            out_ref[:, heads_of(i + j, 1)] = normed.astype(BF16)


def norm_part(place, o, b, n_sub, n_band, queries, intra, prefix, gain, sibs, normed, *deps):
    rows, width = queries.shape
    part = prefix.shape[0] // n_band
    per = 4 if part % 4 == 0 else 1
    size = 2 if per % 2 == 0 else 1
    steps = part // per

    def which(t):
        return (lax.rem(t[3] - o + n_sub, n_sub) * n_band + b) * steps

    cols = pl.BlockSpec((rows, per * DH), lambda i, t: (0, which(t) + i))
    mat = pl.BlockSpec((per, DH, DH), lambda i, t: (which(t) + i, 0, 0))
    in_specs = [
        cols,
        pl.BlockSpec((rows, per * DH), lambda i, t: (0, i)),
        pl.BlockSpec((per, DH, DH), lambda i, t: (b * steps + i, 0, 0)),
        pl.BlockSpec((per, 1, DH), lambda i, t: (which(t) + i, 0, 0)),
    ] + [mat] * len(sibs)
    operands = [queries, intra, prefix, gain, *sibs, *deps]
    in_specs += [ANY] * len(deps)
    aliases = {}
    if normed is not None:
        in_specs.append(ANY)
        operands.append(normed)
        aliases = {len(operands): 0}
    return pl.pallas_call(
        functools.partial(norm_kernel, per, size, n_sub, o),
        grid_spec=pltpu.PrefetchScalarGridSpec(
            num_scalar_prefetch=1,
            grid=(steps,),
            in_specs=in_specs,
            out_specs=[cols, pl.BlockSpec((8, LANES), lambda i, t: (0, 0))],
        ),
        out_shape=[
            jax.ShapeDtypeStruct((rows, width), BF16),
            jax.ShapeDtypeStruct((8, LANES), F32),
        ],
        input_output_aliases=aliases,
        compiler_params=params(ATTN_MIB),
        cost_estimate=cost(1.8),
        name="norm_part",
    )(place, *operands)


class Plan:
    def __init__(self, sizes, cols):
        self.n_group, self.n_ctx, self.n_head, self.n_sub = (
            sizes[a] for a in ("groups", "ctx", "head", "sub")
        )
        self.near = self.n_ctx // self.n_head
        self.split = self.n_group if cols % (self.n_group * LANES) == 0 else 1
        self.rounds = cols // (self.split * LANES)
        self.tiles = self.split * self.rounds
        self.line = self.n_head == 2 and self.near == 2

    def own(self, place):
        return jnp.bitwise_xor(place[1] // self.near, place[2])

    def mine(self, place, step):
        r, _, o, _ = step
        return lax.rem(place[0] + (self.n_group - o), self.split) * self.rounds + r

    def target(self, place, step, j):
        low = jnp.bitwise_xor(lax.rem(place[1], self.near), step[1])
        if self.line:
            far = jnp.where(place[1] < self.near, step[1], self.near - 1 - step[1])
            low = jnp.where(self.own(place) == 0, low, far)
        sub = lax.rem(place[3] + (self.n_sub - j), self.n_sub)
        return (low * self.n_sub + sub) * self.tiles + self.mine(place, step)

    def holder(self, place, step, kh, j):
        low = jnp.bitwise_xor(lax.rem(place[1], self.near), step[1])
        far = jnp.where(place[1] < self.near, step[1], self.near - 1 - step[1])
        half = place[1] // self.near
        ctx = half * self.near + low if kh == 0 else (1 - half) * self.near + far
        group = lax.rem(place[0] + (self.n_group - step[2]), self.split)
        sub = lax.rem(place[3] + (self.n_sub - j), self.n_sub)
        return (group * self.n_ctx + ctx) * self.n_sub + sub


def lanes(i, count):
    return pl.ds(pl.multiple_of(i * LANES, LANES), count * LANES)


def add_up(plan, step, place, stage, keep_hbm, recv_hbm, out_hbm, sems):
    keep, recv, total = stage
    ins = [pltpu.make_async_copy(keep_hbm, keep, sems.at[0])]
    ins += [
        pltpu.make_async_copy(r, recv.at[i], sems.at[1 + i]) for i, r in enumerate(recv_hbm)
    ]
    outs = [
        pltpu.make_async_copy(
            total.at[:, j * step[3] * LANES : (j + 1) * step[3] * LANES],
            out_hbm.at[:, lanes(plan.target(place, step, j), step[3])],
            sems.at[plan.n_head + j],
        )
        for j in range(plan.n_sub)
    ]

    def middle():
        for copy in ins:
            copy.wait()
        value = keep[...]
        for i in range(len(recv_hbm)):
            value = value + recv[i].astype(F32)
        total[...] = value.astype(BF16)
        for copy in outs:
            copy.start()

    def last():
        for copy in outs:
            copy.wait()

    for copy in ins:
        copy.start()
    return middle, last


def project_kernel(plan, step, which, kinds, before, n_deps, place, x, *refs):
    n_head, n_sub = plan.n_head, plan.n_sub
    refs = list(refs)

    def take(n):
        got = refs[:n]
        del refs[:n]
        return got

    w_hbm = take(len(kinds))
    if before is not None:
        keep_old, recv_old = take(1)[0], take(n_head - 1)
    take(n_deps)
    if before is not None:
        take(1 if before[1] else 0)
    res_hbm = take(len(which))
    if before is not None:
        out_hbm = take(1)[0]
    w, keep, send, old_keep, old_recv, total, w_sem, res_sem, old_sem = refs
    rows = x.shape[0]
    tiles = [slice(j * step[3] * LANES, (j + 1) * step[3] * LANES) for j in range(n_sub)]
    tile = 512 if rows % 512 == 0 else rows
    own = plan.own(place)
    loads = []
    for i in range(n_head * n_sub):
        if kinds[0] == 3:
            src = w_hbm[0].at[plan.holder(place, step, i // n_sub, i % n_sub)]
        else:
            src = w_hbm[i]
            if kinds[i]:
                src = src.at[:, lanes(plan.mine(place, step), step[3])]
        dst = w.at[i // n_sub, :, tiles[i % n_sub]]
        loads.append(pltpu.make_async_copy(src, dst, w_sem.at[i]))
    parts = [slice(at, at + tile) for at in range(0, rows, tile)]
    for copy in loads:
        copy.start()
    if before is not None:
        stage = (old_keep, old_recv, total)
        middle, last = add_up(
            plan, before[0], place, stage, keep_old, recv_old, out_hbm, old_sem
        )
    results = []
    for n, o in enumerate(which):
        slot = jnp.bitwise_xor(own, o)
        for j in range(n_sub):
            dst = w.at[slot, :, tiles[j]]
            pltpu.make_async_copy(dst, dst, w_sem.at[slot * n_sub + j]).wait()
        for p in parts:
            res = dot(x[p], w[slot])
            if o == 0:
                keep[p] = res
            else:
                send[o - 1, p] = res.astype(BF16)
        src = keep if o == 0 else send.at[o - 1]
        results.append(pltpu.make_async_copy(src, res_hbm[n], res_sem.at[o]))
        results[-1].start()
        if before is not None and n == 0:
            middle()
    for o in range(n_head):
        if o not in which:
            slot = jnp.bitwise_xor(own, o)
            for j in range(n_sub):
                dst = w.at[slot, :, tiles[j]]
                pltpu.make_async_copy(dst, dst, w_sem.at[slot * n_sub + j]).wait()
    for copy in results:
        copy.wait()
    if before is not None:
        last()


def project(plan, place, step, which, normed, pieces, before, out, deps):
    rows, depth = normed.shape
    n_head, n_sub = plan.n_head, plan.n_sub
    width = n_sub * step[3] * LANES
    kinds = [3 if p.ndim == 3 else int(p.shape[1] != step[3] * LANES) for p in pieces]
    operands = [normed, *pieces]
    shapes = [jax.ShapeDtypeStruct((rows, width), BF16 if o else F32) for o in which]
    aliases, info = {}, None
    if before is not None:
        operands += [before[1], *before[2]]
        info = (before[0], out is not None)
    operands += deps
    if before is not None:
        shapes.append(jax.ShapeDtypeStruct((rows, n_sub * plan.near * plan.tiles * LANES), BF16))
        if out is not None:
            operands.append(out)
            aliases = {len(operands): len(shapes) - 1}
    old = width if before is None else n_sub * before[0][3] * LANES
    dma = pltpu.SemaphoreType.DMA
    return pl.pallas_call(
        functools.partial(project_kernel, plan, step, which, kinds, info, len(deps)),
        in_specs=[
            pl.BlockSpec(memory_space=pltpu.SMEM),
            pl.BlockSpec(memory_space=pltpu.VMEM),
            *[ANY] * (len(operands) - 1),
        ],
        out_specs=[ANY] * len(shapes),
        scratch_shapes=[
            pltpu.VMEM((n_head, depth, width), BF16),
            pltpu.VMEM((rows, width), F32),
            pltpu.VMEM((max(1, n_head - 1), rows, width), BF16),
            pltpu.VMEM((rows, old), F32),
            pltpu.VMEM((max(1, n_head - 1), rows, old), BF16),
            pltpu.VMEM((rows, old), BF16),
            dma((n_head * n_sub,)),
            dma((n_head,)),
            dma((n_head + n_sub,)),
        ],
        out_shape=shapes,
        input_output_aliases=aliases,
        compiler_params=params(32),
        cost_estimate=cost(4),
        name="project",
    )(place, *operands)


def combine_kernel(plan, step, n_recv, place, *refs):
    keep_hbm, recv_hbm = refs[0], refs[1 : 1 + n_recv]
    out_hbm, keep, recv, total, sems = refs[-5:]
    middle, last = add_up(
        plan, step, place, (keep, recv, total), keep_hbm, recv_hbm, out_hbm, sems
    )
    middle()
    last()


def combine(plan, place, step, keep, recvs, out):
    rows, width = keep.shape
    operands = [keep, *recvs, out]
    return pl.pallas_call(
        functools.partial(combine_kernel, plan, step, len(recvs)),
        grid_spec=pltpu.PrefetchScalarGridSpec(
            num_scalar_prefetch=1,
            grid=(1,),
            in_specs=[ANY] * len(operands),
            out_specs=ANY,
            scratch_shapes=[
                pltpu.VMEM((rows, width), F32),
                pltpu.VMEM((max(1, len(recvs)), rows, width), BF16),
                pltpu.VMEM((rows, width), BF16),
                pltpu.SemaphoreType.DMA((plan.n_head + plan.n_sub,)),
            ],
        ),
        out_shape=jax.ShapeDtypeStruct(out.shape, BF16),
        input_output_aliases={len(operands): 0},
        compiler_params=params(),
        cost_estimate=cost(0.5),
        name="combine",
    )(place, *operands)


def shift(x, axis, size, o):
    return lax.ppermute(x, axis, [(i, (i + o) % size) for i in range(size)])


def swap(x, axis, size, k):
    return lax.ppermute(x, axis, [(i, i ^ k) for i in range(size)])


def local(sizes, queries, keys, values, out_weight, norm_gain):
    rows, width = queries.shape
    heads = width // DH
    depth, cols = out_weight.shape
    plan = Plan(sizes, cols)
    n_group, n_ctx, n_head, n_sub = plan.n_group, plan.n_ctx, plan.n_head, plan.n_sub
    near, split, rounds = plan.near, plan.split, plan.rounds
    place = jnp.stack([lax.axis_index(a) for a in ("groups", "ctx", "head", "sub")]).astype(jnp.int32)
    s = place[3]

    steps = [(r, kl, o, 1) for r in range(rounds) for kl in range(near) for o in range(split)]
    line = plan.line and rounds == 2 and split == 2

    whole = [out_weight] + [shift(out_weight, "sub", n_sub, j) for j in range(1, n_sub)]

    def cut(r, where):
        at = plan.mine(where, (r, 0, 0, 1)) * LANES
        return lax.dynamic_slice(out_weight, (0, at), (depth, LANES))

    first = [cut(0, place)]
    pieces = {(r, 0, o, 1, 0): whole for r in range(rounds) for o in range(split)}
    later = {}
    held = {step: [] for step in steps}

    def cross(piece):
        return [piece] + [shift(piece, "sub", n_sub, j) for j in range(1, n_sub)]

    def hold(n, *arrays):
        held[steps[n]] += arrays

    part = heads // n_sub
    states, sent = block_states(keys, values, heads, first[0])
    sibs = [shift(sent, "sub", n_sub, o) for o in range(1, n_sub)]
    total = sum(
        lax.dynamic_slice_in_dim(x, s * part, part).astype(F32) for x in [states, *sibs]
    )
    ends, middle, out_way = [(0, 1), (1, 0), (2, 3), (3, 2)], [(1, 2), (2, 1)], [(1, 0), (2, 3)]
    prefix = jnp.zeros((part, DH, DH), BF16)
    n_band = 1
    bands = [(o, b) for o in range(n_sub) for b in range(n_band)]
    intra, tokens = {}, []
    for i in range(n_ctx - 1):
        hop = (prefix.astype(F32) + total).astype(BF16)
        if i < len(bands):
            deps = [hop] if i == 0 else [hop, *whole[1:]]
            intra[bands[i]], token = intra_block(
                place, *bands[i], n_sub, n_band, queries, keys, values, part, *deps
            )
            tokens.append(token)
        moved = lax.ppermute(hop, "ctx", [(i, i + 1)])
        prefix = prefix + (gate(moved, tokens[i]) if i < len(tokens) else moved)
    first += [cut(r, gate(place, tokens[0])) for r in range(1, rounds)]
    gain = norm_gain.reshape(heads, 1, DH)

    normed, normed_token = None, None
    for o in range(n_sub):
        mat = prefix if o == 0 else shift(prefix, "sub", n_sub, o)
        for b in range(n_band):
            deps = []
            normed, token = norm_part(
                place, o, b, n_sub, n_band, queries, intra[o, b], mat, gain, sibs, normed, *deps
            )
            normed_token = token if normed_token is None else normed_token

    if line:
        inner = (place[1] == 1) | (place[1] == 2)

        def along(x, perm, *deps):
            return lax.ppermute(gate(x, *deps) if deps else x, "ctx", perm)

        def over(x, *deps):
            return shift(gate(x, *deps) if deps else x, "groups", n_group, 1)

        near_a = gate(along(first[0], ends), tokens[0])
        across_a = gate(along(first[0], middle), tokens[0])
        y_near_a = over(near_a)
        outward_a = gate(along(across_a, out_way), tokens[1])
        across_b = gate(along(near_a, middle), tokens[1])
        outward_b = along(across_b, out_way, prefix)
        far_a = jnp.where(inner, across_a, outward_a)
        far_b = jnp.where(inner, across_b, outward_b)
        y_far_a = over(far_a, prefix)
        pieces[0, 0, 0, 1, 1] = cross(far_a)
        pieces[0, 0, 1, 1, 1] = cross(y_far_a)
        hold(1, y_near_a, outward_b)

        def after_0(*sent):
            later["across_c"] = along(first[1], middle, *sent)
            later["near_c"] = along(first[1], ends, *sent)
            later["y_far_b"] = over(gate(far_b, *sent))
            pieces[0, 1, 0, 1, 0] = cross(gate(near_a, *sent))
            pieces[0, 1, 0, 1, 1] = cross(gate(far_b, *sent))
            hold(2, later["across_c"], later["near_c"], later["y_far_b"])

        def after_1(*sent):
            later["outward_c"] = along(later["across_c"], out_way, *sent)
            later["across_d"] = along(later["near_c"], middle, *sent)
            later["y_near_c"] = over(later["near_c"], later["y_far_b"])
            pieces[0, 1, 1, 1, 0] = cross(gate(y_near_a, *sent))
            pieces[0, 1, 1, 1, 1] = cross(later["y_far_b"])
            hold(3, later["outward_c"], later["across_d"], later["y_near_c"])

        def after_2(*sent):
            far_c = jnp.where(inner, later["across_c"], later["outward_c"])
            pieces[1, 0, 0, 1, 1] = cross(far_c)
            later["y_far_c"] = over(far_c, later["y_near_c"])
            outward_d = along(later["across_d"], out_way)
            far_d = jnp.where(inner, later["across_d"], outward_d)
            pieces[1, 0, 1, 1, 1] = cross(later["y_far_c"])
            y_far_d = over(far_d, later["y_far_c"])
            hold(4, later["y_far_c"], outward_d)
            pieces[1, 1, 0, 1, 0] = cross(gate(later["near_c"], *sent))
            pieces[1, 1, 0, 1, 1] = cross(far_d)
            pieces[1, 1, 1, 1, 0] = cross(gate(later["y_near_c"], *sent))
            pieces[1, 1, 1, 1, 1] = cross(y_far_d)
            hold(4, *pieces[1, 1, 0, 1, 0][1:])
            hold(5, *pieces[1, 1, 0, 1, 1][1:], *pieces[1, 1, 1, 1, 0][1:])
            hold(6, y_far_d)

        later = {0: after_0, 1: after_1, 2: after_2}
    else:
        for r in range(rounds):
            for kl in range(near):
                for kh in range(n_head):
                    if kl or kh:
                        piece = swap(first[r], "ctx", n_ctx, kh * near + kl)
                        pieces[r, kl, 0, 1, kh] = cross(piece)
                        for o in range(1, split):
                            pieces[r, kl, o, 1, kh] = cross(shift(piece, "groups", n_group, o))

    out, sent, late = None, [], None
    waiting = []
    others = list(range(1, n_head))
    for n, step in enumerate(steps):
        use = [p for kh in range(n_head) for p in pieces[*step, kh]]
        before = waiting.pop(0) if len(waiting) > 1 else None
        which = others if n == 0 and len(steps) > 1 else others + [0]
        deps = held[step] + sent
        shares = list(project(plan, place, step, which, normed, use, before, out, deps))
        if before is not None:
            out = shares.pop()
        got = dict(zip(which, shares))
        sent = shares[:1]
        if late:
            waiting[0] = late(sent)
            late = None
        recvs = [swap(got[i], "head", n_head, i) for i in others]
        waiting.append((step, got.get(0), recvs))
        if n in later:
            later[n](*sent)
        if 0 not in got:

            def late(deps, step=step, use=use, recvs=recvs):
                return step, project(plan, place, step, [0], normed, use, None, None, deps)[0], recvs

    if out is None:
        out = jnp.zeros((rows, n_sub * near * cols), BF16)
    for step, keep, recvs in waiting:
        out = combine(plan, place, step, keep, recvs, out)
    return out


def solution(mesh):
    return jax.shard_map(
        functools.partial(local, dict(mesh.shape)),
        mesh=mesh,
        in_specs=(
            P(("groups", "ctx", "sub"), "head"),
            P(("groups", "ctx", "sub"), "head"),
            P(("groups", "ctx", "sub"), "head"),
            P("head", ("ctx", "sub")),
            P("head"),
        ),
        out_specs=P(("groups", "ctx", "sub"), "head"),
        check_vma=False,
    )
```
